128 devices in a mesh: row: 8 (over y, core), col: 16 (over x, z).
Axes of the slice: x: 4, y: 4, z: 4, core: 2. Of those that a mesh axis runs over, the one named last changes fastest.
Arguments:
- x_blocks: bfloat16 [8, 16, 16, 128, 1024], P('row', 'col'), may hold values from -6 to 6
- factors: bfloat16 [8, 16, 16, 11, 2, 128, 128], P('row', 'col'), may hold values from -0.375 to 0.375
- pattern: int32 [8, 16, 16, 11], P('row', 'col'), may hold values 0 or 1
Outputs:
- result: bfloat16 [8, 16, 16, 128, 1024], P('row', 'col')
The draws below stay inside these ranges and needn't reach their ends.
All inputs are finite; a program needn't handle non-finite values. No bound on the sum of `pattern` on one device may be relied on, other than what follows from the above.
Results may differ from the reference program's by a relative error of at most 0.02.
Values may be sent and summed in bfloat16 or wider, within the bound.
A program may use at most 128 MiB of HBM per device.

```python
import jax
import jax.numpy as jnp

B = 128
R = 1024
BD = 16
LEVELS = 11
N_ROW = 8
N_COL = 16


def place_ends(drawn, own_key, low, high):
    dims = drawn.shape
    index_at = [jax.random.randint(jax.random.fold_in(own_key, axis), (), 0, dims[axis]) for axis in range(len(dims))]
    drawn = drawn.at[tuple(index_at)].set(low)
    longest = dims.index(max(dims))
    index_at[longest] = (index_at[longest] + 1) % dims[longest]
    return drawn.at[tuple(index_at)].set(high)


def shard_levels(key, dims, shards, least, largest):
    def one(axis_at, blocks):
        draws = jax.random.uniform(jax.random.fold_in(jax.random.fold_in(key, 6), axis_at), (blocks,), jnp.float32, least / len(shards), largest / len(shards))
        return jnp.repeat(jnp.exp(draws), dims[axis_at] // blocks).reshape((-1,) + (1,) * (len(dims) - axis_at - 1))

    level = one(*shards[0])
    for cut in shards[1:]:
        level = level * one(*cut)
    return level


def centred(stream_key, shape, spread, reach, split=(), held_as=jnp.bfloat16):
    factor_of = shard_levels(stream_key, shape, split, -0.22, 0.18) if split else 1.0
    values = jax.random.normal(stream_key, shape, jnp.float32) * spread * factor_of
    return jnp.minimum(jnp.maximum(values, -reach), reach).astype(held_as)


def setup_inputs(seed: int = 0) -> dict:
    arg_keys = jax.random.split(jax.random.key(seed), 4)
    x_blocks = centred(arg_keys[0], (N_ROW, N_COL, BD, B, R), 1.0, 6.0, ((0, 8), (1, 16)))
    factors = centred(arg_keys[1], (N_ROW, N_COL, BD, LEVELS, 2, B, B), (7 * B // 4) ** -0.5, 0.375, ((0, 8), (1, 16)))
    pattern = place_ends((jax.random.randint(arg_keys[2], (N_ROW, N_COL, BD, LEVELS), 0, 4) < 3).astype(jnp.int32), jax.random.fold_in(arg_keys[2], 1), 0, 1)
    return dict(x_blocks=x_blocks, factors=factors, pattern=pattern)


def reference(x_blocks, factors, pattern):
    count = N_ROW * N_COL * BD
    values = x_blocks.reshape(count, B, R)
    weights = factors.reshape(count, LEVELS, 2, B, B)
    active = pattern.reshape(count, LEVELS)
    for level in range(LEVELS):
        span = 2 ** level
        partner = values.reshape(count // (2 * span), 2, span, B, R)[:, ::-1].reshape(count, B, R)
        level_w = weights[:, level].astype(jnp.float32)
        own = jnp.einsum("nij,njr->nir", level_w[:, 0], values.astype(jnp.float32))
        cross = jnp.einsum("nij,njr->nir", level_w[:, 1], partner.astype(jnp.float32))
        values = (own + active[:, level].astype(jnp.float32)[:, None, None] * cross).astype(jnp.bfloat16)
    return values.reshape(N_ROW, N_COL, BD, B, R)
```

```python
import functools

import jax
import jax.numpy as jnp
from jax import lax
from jax.experimental import pallas as pl
from jax.experimental.pallas import tpu as pltpu
from jax.sharding import PartitionSpec as P

MESH = pl.DeviceIdType.MESH
B = 128
W = 128
WL = 256
GROUPS = 4
DEPTH = 4
OFF = (0, 2, 4, 6, 8, 10, 12, 14)


def dot(lhs, rhs):
    return jnp.dot(lhs, rhs, preferred_element_type=jnp.float32).astype(jnp.bfloat16)


def side(p):
    return lax.rem(lax.rem(p, 2) + lax.div(p, 2), 2)


def flip(p):
    return p + 1 - 2 * lax.rem(p, 2)


def kernel(
    pat, x_hbm, f_hbm, out, H, FAC, FRZ, FRX, FRC, FRY,
    R1, R2, R3, R4, R5, R6, R7, S1, S2, S3, S4, S5, S6, S7,
    xs, fs, frs, fss,
    r1, r2, r3, r4, r5, r6, r7, r8, s1, s2, s3, s4, s5, s6, s7, s8, os,
):
    width = H.shape[4]
    chunks = width // W
    units = GROUPS * chunks
    row = lax.axis_index("row")
    col = lax.axis_index("col")
    y, c = lax.div(row, 2), lax.rem(row, 2)
    xx, z = lax.div(col, 4), lax.rem(col, 4)
    sz, sx, sy = side(z), side(xx), side(y)

    def dev(z_, x_, y_, c_):
        return (y_ * 2 + c_, x_ * 4 + z_)

    fz, fx, fy, fc = flip(z), flip(xx), flip(y), 1 - c
    Z1, Z3 = dev(fz, xx, y, c), dev(3 - z, xx, y, c)
    X1, X3 = dev(z, fx, y, c), dev(z, 3 - xx, y, c)
    Y1, Y3 = dev(z, xx, fy, c), dev(z, xx, 3 - y, c)
    C1 = dev(z, xx, y, fc)
    ZX, XC, YC = dev(fz, fx, y, c), dev(z, fx, y, fc), dev(z, xx, fy, fc)

    def send(src, dst, ssem, rsem, to):
        return pltpu.make_async_remote_copy(
            src_ref=src, dst_ref=dst, send_sem=ssem, recv_sem=rsem, device_id=to, device_id_type=MESH
        )

    def load_f(k):
        return pltpu.make_async_copy(f_hbm.at[:, k], FAC.at[:, k], fs.at[k])

    def load_x(i):
        cols = pl.ds(i * WL, WL)
        return pltpu.make_async_copy(x_hbm.at[:, :, :, :, cols], H.at[:, :, :, :, cols], xs.at[i])

    for k in (4, 5, 0):
        load_f(k).start()
    load_x(0).start()
    for k in (1, 2, 3):
        load_f(k).start()
    for i in range(1, width // WL):
        load_x(i).start()
    for k in (6, 7, 8, 9, 10):
        load_f(k).start()

    barrier = pltpu.get_barrier_semaphore()
    partners = (Z1, Z3, ZX, X1, X3, XC, C1, YC, Y1, Y3)
    for to in partners:
        pl.semaphore_signal(barrier, inc=1, device_id=to, device_id_type=MESH)

    def scale(levels):
        def body(l, carry):
            for k in levels:
                m = pat[0, 0, l, k].astype(jnp.float32)
                FAC[l, k, 1] = (FAC[l, k, 1].astype(jnp.float32) * m).astype(jnp.bfloat16)
            return carry

        lax.fori_loop(0, 4 * GROUPS, body, 0)

    def f_z(g, j):
        return send(
            FAC.at[4 * g + 2 * j + 1 - sz, 4:6], FRZ.at[g, j], fss.at[0, g, j], frs.at[0, g, j], Z1
        )

    def f_x(g, j):
        return send(
            FAC.at[4 * g + 2 * (1 - sx) + j, 6:8], FRX.at[g, j], fss.at[1, g, j], frs.at[1, g, j], X1
        )

    def f_c(g, j):
        return send(
            FAC.at[4 * g + 2 * j + 1 - c, 8], FRC.at[g, j], fss.at[2, g, j], frs.at[2, g, j], C1
        )

    def f_y(g, j):
        return send(
            FAC.at[4 * g + 2 * (1 - sy) + j, 9:11], FRY.at[g, j], fss.at[3, g, j], frs.at[3, g, j], Y1
        )

    def pair(fo, fx_, vo, vx):
        lhs = jnp.concatenate(
            [jnp.concatenate([fo[0], fo[1]], axis=1), jnp.concatenate([fx_[1], fx_[0]], axis=1)], axis=0
        )
        res = dot(lhs, jnp.concatenate([vo, vx], axis=0))
        return res[:B], res[B:]

    def one(f, v, w):
        return dot(jnp.concatenate([f[0], f[1]], axis=1), jnp.concatenate([v, w], axis=0))

    def local(i):
        cols = pl.ds(pl.multiple_of(i * WL, WL), WL)
        for k in range(4):
            span = 2**k

            def body(n, carry, k=k, span=span):
                la = lax.div(n, span) * (2 * span) + lax.rem(n, span)
                lb = la + span
                ia = (lax.div(la, 4), lax.rem(lax.div(la, 2), 2), lax.rem(la, 2))
                ib = (lax.div(lb, 4), lax.rem(lax.div(lb, 2), 2), lax.rem(lb, 2))
                va, vb = H[ia[0], ia[1], ia[2], :, cols], H[ib[0], ib[1], ib[2], :, cols]
                oa, ob = pair((FAC[la, k, 0], FAC[la, k, 1]), (FAC[lb, k, 0], FAC[lb, k, 1]), va, vb)
                H[ia[0], ia[1], ia[2], :, cols] = oa
                H[ib[0], ib[1], ib[2], :, cols] = ob
                return carry

            lax.fori_loop(0, 2 * GROUPS, body, 0)

    load_f(4).wait()
    load_f(5).wait()
    scale((4, 5))
    pl.semaphore_wait(barrier, len(partners))
    for j in range(2):
        f_z(0, j).start()
    for k in range(4):
        load_f(k).wait()
    scale((0, 1, 2, 3))
    load_x(0).wait()
    local(0)

    def place(u):
        g, cc = lax.div(u, chunks), lax.rem(u, chunks)
        return g, cc, pl.ds(pl.multiple_of(cc * W, W), W), lax.rem(u, DEPTH)

    def c1(u):
        g, cc, cols, d = place(u)
        return [send(H.at[g, :, 1 - sz, :, cols], R1.at[u], s1.at[d], r1.at[u], Z1)]

    def c2(u):
        d = lax.rem(u, DEPTH)
        return [send(S1.at[d], R2.at[u], s2.at[d], r2.at[u], Z3)]

    def turn(S, R, ss, rs, u, keep, to):
        d = lax.rem(u, DEPTH)
        return [
            send(S.at[d, 1, keep], R.at[u, 0], ss.at[d, 0], rs.at[u, 0], to[0]),
            send(S.at[d, 0, 1 - keep], R.at[u, 1], ss.at[d, 1], rs.at[u, 1], to[1]),
            send(S.at[d, 1, 1 - keep], R.at[u, 2], ss.at[d, 2], rs.at[u, 2], to[2]),
        ]

    kx = sx
    kc = lax.rem(c + sz, 2)
    ky = lax.rem(sx + sy, 2)

    def c3(u):
        return turn(S2, R3, s3, r3, u, kx, (Z1, X1, ZX))

    def c4(u):
        d = lax.rem(u, DEPTH)
        return [send(S3.at[d], R4.at[u], s4.at[d], r4.at[u], X3)]

    def c5(u):
        return turn(S4, R5, s5, r5, u, kc, (X1, C1, XC))

    def c6(u):
        return turn(S5, R6, s6, r6, u, ky, (C1, Y1, YC))

    def c7(u):
        d = lax.rem(u, DEPTH)
        return [send(S6.at[d], R7.at[u], s7.at[d], r7.at[u], Y3)]

    def b0(i):
        return c if i == 0 else 1 - c

    def c8(u):
        g, cc, cols, d = place(u)
        return [
            send(S7.at[d, 1, i], out.at[g, sy, b0(i), :, cols], s8.at[d, i], r8.at[u, i], Y1)
            for i in range(2)
        ]

    def co(u):
        g, cc, cols, d = place(u)
        return [
            pltpu.make_async_copy(S7.at[d, 0, i], out.at[g, sy, b0(i), :, cols], os.at[d, i])
            for i in range(2)
        ]

    def start(copies):
        for copy in copies:
            copy.start()

    def received(copies):
        for copy in copies:
            copy.wait_recv()

    def reuse(u, make):
        @pl.when(u >= DEPTH)
        def _():
            for copy in make(u):
                copy.wait_send()

    def factors_in(u, make):
        g, cc = lax.div(u, chunks), lax.rem(u, chunks)

        @pl.when(cc == 0)
        def _():
            for j in range(2):
                make(g, j).wait_recv()

    def exchange(u, Sin, Rin, Sout, own, oth):
        d = lax.rem(u, DEPTH)
        for i in range(2):
            fo, fx_ = own(i), oth(i)
            Sout[d, 0, i] = one(fo, Sin[d, 0, i], Rin[u, 1, i])
            Sout[d, 1, i] = one(fx_, Sin[d, 1, i], Rin[u, 0, i])

    def both(u, Sin, keep, Rin, first, Sout, own, oth):
        d = lax.rem(u, DEPTH)
        a, b = pair(own(0), oth(0), Sin[d, 0, keep], Rin[u, 1])
        Sout[d, 0, 0] = a
        Sout[d, 1, 0] = b
        a, b = pair(own(1), oth(1), Rin[u, 0], Rin[u, 2])
        Sout[d, 0, 1] = a
        Sout[d, 1, 1] = b

    def stage_z0(u):
        g, cc, cols, d = place(u)
        factors_in(u, f_z)
        reuse(u, c2)
        received(c1(u))
        for j in range(2):
            l = 4 * g + 2 * j + sz
            a, b = pair(
                (FAC[l, 4, 0], FAC[l, 4, 1]), (FRZ[g, j, 0, 0], FRZ[g, j, 0, 1]),
                H[g, j, sz, :, cols], R1[u, j],
            )
            S1[d, 0, j] = a
            S1[d, 1, j] = b
        start(c2(u))

    def stage_z1(u):
        g = lax.div(u, chunks)
        reuse(u, c3)
        received(c2(u))
        exchange(
            u, S1, R2, S2,
            lambda j: (FAC[4 * g + 2 * j + sz, 5, 0], FAC[4 * g + 2 * j + sz, 5, 1]),
            lambda j: (FRZ[g, j, 1, 0], FRZ[g, j, 1, 1]),
        )
        start(c3(u))

    def z_of(i):
        return sz if i == 0 else 1 - sz

    def stage_x0(u):
        g = lax.div(u, chunks)
        factors_in(u, f_x)
        reuse(u, c4)
        received(c3(u))
        both(
            u, S2, kx, R3, sz, S3,
            lambda i: (FAC[4 * g + 2 * sx + z_of(i), 6, 0], FAC[4 * g + 2 * sx + z_of(i), 6, 1]),
            lambda i: (FRX[g, z_of(i), 0, 0], FRX[g, z_of(i), 0, 1]),
        )
        start(c4(u))

    def stage_x1(u):
        g = lax.div(u, chunks)
        reuse(u, c5)
        received(c4(u))
        exchange(
            u, S3, R4, S4,
            lambda i: (FAC[4 * g + 2 * sx + z_of(i), 7, 0], FAC[4 * g + 2 * sx + z_of(i), 7, 1]),
            lambda i: (FRX[g, z_of(i), 1, 0], FRX[g, z_of(i), 1, 1]),
        )
        start(c5(u))

    def x_of(i):
        return sx if i == 0 else 1 - sx

    def stage_c(u):
        g = lax.div(u, chunks)
        factors_in(u, f_c)
        reuse(u, c6)
        received(c5(u))
        both(
            u, S4, kc, R5, sx, S5,
            lambda i: (FAC[4 * g + 2 * x_of(i) + c, 8, 0], FAC[4 * g + 2 * x_of(i) + c, 8, 1]),
            lambda i: (FRC[g, x_of(i), 0], FRC[g, x_of(i), 1]),
        )
        start(c6(u))

    def stage_y0(u):
        g = lax.div(u, chunks)
        factors_in(u, f_y)
        reuse(u, c7)
        received(c6(u))
        both(
            u, S5, ky, R6, c, S6,
            lambda i: (FAC[4 * g + 2 * sy + b0(i), 9, 0], FAC[4 * g + 2 * sy + b0(i), 9, 1]),
            lambda i: (FRY[g, b0(i), 0, 0], FRY[g, b0(i), 0, 1]),
        )
        start(c7(u))

    def stage_y1(u):
        g = lax.div(u, chunks)
        reuse(u, c8)

        @pl.when(u >= DEPTH)
        def _():
            for copy in co(u):
                copy.wait()

        received(c7(u))
        exchange(
            u, S6, R7, S7,
            lambda i: (FAC[4 * g + 2 * sy + b0(i), 10, 0], FAC[4 * g + 2 * sy + b0(i), 10, 1]),
            lambda i: (FRY[g, b0(i), 1, 0], FRY[g, b0(i), 1, 1]),
        )
        start(c8(u))
        start(co(u))

    def stage_swap(u):
        reuse(u, c1)
        start(c1(u))
        g, cc = lax.div(u, chunks), lax.rem(u, chunks)

        @pl.when(jnp.logical_and(g < GROUPS - 1, lax.rem(cc, 4) == 1))
        def _():
            f_z(g + 1, lax.div(cc, 4)).start()

    stages = (stage_swap, stage_z0, stage_z1, stage_x0, stage_x1, stage_c, stage_y0, stage_y1)

    def step(t, carry):
        for off, stage in zip(OFF, stages):
            @pl.when(jnp.logical_and(t >= off, t < off + units))
            def _(off=off, stage=stage):
                stage(t - off)

            if stage is stage_swap:
                @pl.when(jnp.logical_and(t < 2 * (width // WL - 1), lax.rem(t, 2) == 0))
                def _():
                    i = lax.div(t, 2) + 1
                    load_x(i).wait()
                    local(i)

                @pl.when(t == 1)
                def _():
                    for k in (6, 7, 8, 9, 10):
                        load_f(k).wait()
                    scale((6, 7, 8, 9, 10))
                    for g in range(GROUPS):
                        for j in range(2):
                            f_x(g, j).start()
                            f_c(g, j).start()
                            f_y(g, j).start()

        return carry

    lax.fori_loop(0, units + OFF[-1], step, 0)

    for u in range(units - DEPTH, units):
        for make in (c1, c2, c3, c4, c5, c6, c7, c8):
            for copy in make(u):
                copy.wait_send()
        for copy in co(u):
            copy.wait()

    def finish(u, carry):
        received(c8(u))
        return carry

    lax.fori_loop(0, units, finish, 0)
    for g in range(GROUPS):
        for j in range(2):
            for make in (f_z, f_x, f_c, f_y):
                make(g, j).wait_send()


def on_device(x_blocks, factors, pattern):
    blocks, order, width = x_blocks.shape[2:]
    levels = factors.shape[3]
    units = GROUPS * (width // W)
    dma = pltpu.SemaphoreType.DMA
    bf = jnp.bfloat16
    tile = (order, W)
    scratch = [
        pltpu.VMEM((GROUPS, 2, 2, order, width), bf),
        pltpu.VMEM((blocks, levels, 2, order, order), bf),
        pltpu.VMEM((GROUPS, 2, 2, 2, order, order), bf),
        pltpu.VMEM((GROUPS, 2, 2, 2, order, order), bf),
        pltpu.VMEM((GROUPS, 2, 2, order, order), bf),
        pltpu.VMEM((GROUPS, 2, 2, 2, order, order), bf),
        pltpu.VMEM((units, 2) + tile, bf),
        pltpu.VMEM((units, 2, 2) + tile, bf),
        pltpu.VMEM((units, 3) + tile, bf),
        pltpu.VMEM((units, 2, 2) + tile, bf),
        pltpu.VMEM((units, 3) + tile, bf),
        pltpu.VMEM((units, 3) + tile, bf),
        pltpu.VMEM((units, 2, 2) + tile, bf),
    ]
    scratch += [pltpu.VMEM((DEPTH, 2, 2) + tile, bf)] * 7
    scratch += [
        dma((width // WL,)), dma((levels,)), dma((4, GROUPS, 2)), dma((4, GROUPS, 2)),
        dma((units,)), dma((units,)), dma((units, 3)), dma((units,)), dma((units, 3)), dma((units, 3)),
        dma((units,)), dma((units, 2)),
        dma((DEPTH,)), dma((DEPTH,)), dma((DEPTH, 3)), dma((DEPTH,)), dma((DEPTH, 3)), dma((DEPTH, 3)),
        dma((DEPTH,)), dma((DEPTH, 2)), dma((DEPTH, 2)),
    ]
    result = pl.pallas_call(
        kernel,
        out_shape=jax.ShapeDtypeStruct((GROUPS, 2, 2, order, width), bf),
        in_specs=[
            pl.BlockSpec(memory_space=pltpu.SMEM),
            pl.BlockSpec(memory_space=pl.ANY),
            pl.BlockSpec(memory_space=pl.ANY),
        ],
        out_specs=pl.BlockSpec(memory_space=pl.ANY),
        scratch_shapes=scratch,
        name="butterfly",
        cost_estimate=pl.CostEstimate(
            flops=blocks * levels * 4 * order * order * width,
            bytes_accessed=2 * (2 * x_blocks.size + factors.size),
            transcendentals=0,
        ),
        compiler_params=pltpu.CompilerParams(
            collective_id=0, has_side_effects=True, vmem_limit_bytes=60 * 2**20
        ),
    )(
        pattern,
        x_blocks.reshape(GROUPS, 2, 2, order, width),
        factors.reshape(blocks, levels, 2, order, order),
    )
    return result.reshape(1, 1, blocks, order, width)


def solution(mesh):
    return jax.shard_map(
        on_device,
        mesh=mesh,
        in_specs=(
            P("row", "col", None, None, None),
            P("row", "col", None, None, None, None, None),
            P("row", "col", None, None),
        ),
        out_specs=P("row", "col", None, None, None),
        check_vma=False,
    )
```

```python
import functools

import jax
import jax.numpy as jnp
from jax import lax
from jax.experimental import pallas as pl
from jax.experimental.pallas import tpu as pltpu
from jax.sharding import PartitionSpec as P

MESH = pl.DeviceIdType.MESH
B = 128
W = 128
WL = 256
RING = 4
BLOCKS = 16
GROUPS = BLOCKS // RING
DEPTH = 4
OFF = (0, 2, 4, 6, 8, 10)
ORDER = (0, 1, 2, 3, 4, 5)


def dot(lhs, rhs):
    return jnp.dot(lhs, rhs, preferred_element_type=jnp.float32).astype(jnp.bfloat16)


def pair(fa, fb, va, vb):
    lhs = jnp.concatenate(
        [jnp.concatenate([fa[0], fa[1]], axis=1), jnp.concatenate([fb[1], fb[0]], axis=1)], axis=0
    )
    res = dot(lhs, jnp.concatenate([va, vb], axis=0))
    return res[:B], res[B:]


def kernel(
    pat, x_hbm, f_hbm, out, H, FAC, FRZ, FRX, FRC, FRY,
    RZ, HZ, RX, RC, RY, SZ, SX, SC, SY,
    xs, fs, frs, fss,
    rz, rh, rx, rc, ry, ro, sh, sz, shx, sx, sc, sy, os,
):
    width = H.shape[2]
    chunks = width // W
    units = GROUPS * chunks
    row = lax.axis_index("row")
    col = lax.axis_index("col")
    y, c = lax.div(row, 2), lax.rem(row, 2)
    x, z = lax.div(col, 4), lax.rem(col, 4)

    def dev(z_, x_, y_, c_):
        return (y_ * 2 + c_, x_ * 4 + z_)

    def far(p, k):
        return lax.rem(p + k, RING)

    HOPS = (2, 1, 3)

    def send(src, dst, ssem, rsem, to):
        return pltpu.make_async_remote_copy(
            src_ref=src, dst_ref=dst, send_sem=ssem, recv_sem=rsem, device_id=to, device_id_type=MESH
        )

    def load_f(k):
        return pltpu.make_async_copy(f_hbm.at[:, k], FAC.at[:, k], fs.at[k])

    def load_fz(g, n):
        part = pl.ds(RING * g, RING * n)
        return pltpu.make_async_copy(
            f_hbm.at[part, 4:6], FAC.at[part, 4:6], fs.at[4 if g == 0 else 5]
        )

    def load_x(i):
        cols = pl.ds(i * WL, WL)
        return pltpu.make_async_copy(x_hbm.at[:, :, cols], H.at[:, :, cols], xs.at[i])

    load_fz(0, 1).start()
    load_x(0).start()
    for k in range(4):
        load_f(k).start()
    load_fz(1, GROUPS - 1).start()
    for i in range(1, width // WL):
        load_x(i).start()
    for k in range(6, 11):
        load_f(k).start()

    barrier = pltpu.get_barrier_semaphore()
    partners = [dev(far(z, k), x, y, c) for k in HOPS]
    partners += [dev(z, far(x, k), y, e) for k in HOPS for e in (c, 1 - c)]
    partners += [dev(z, x, far(y, k), e) for k in HOPS for e in (c, 1 - c)]
    partners += [dev(z, x, y, 1 - c)]
    for to in partners:
        pl.semaphore_signal(barrier, inc=1, device_id=to, device_id_type=MESH)

    def scale(first, count, levels):
        def body(l, carry):
            for k in levels:
                m = pat[0, k, 0, l].astype(jnp.float32)
                FAC[l, k, 1] = (FAC[l, k, 1].astype(jnp.float32) * m).astype(jnp.bfloat16)
            return carry

        lax.fori_loop(first, first + count, body, 0)

    def f_z(g, k, n):
        q = far(z, k)
        return send(
            FAC.at[RING * g + q, 4 + n], FRZ.at[g, z, n], fss.at[0, g, k, n], frs.at[0, g, z, n],
            dev(q, x, y, c),
        )

    def f_z_in(g, k, n):
        p = far(z, k)
        return send(
            FAC.at[RING * g + p, 4 + n], FRZ.at[g, p, n], fss.at[0, g, k, n], frs.at[0, g, p, n],
            dev(p, x, y, c),
        )

    def f_x(g, k):
        q = far(x, k)
        return send(
            FAC.at[RING * g + q, 6:8], FRX.at[g, x], fss.at[1, g, k, 0], frs.at[1, g, x, 0], dev(z, q, y, c)
        )

    def f_x_in(g, k):
        p = far(x, k)
        return send(
            FAC.at[RING * g + p, 6:8], FRX.at[g, p], fss.at[1, g, k, 0], frs.at[1, g, p, 0], dev(z, p, y, c)
        )

    def f_y(g, k):
        q = far(y, k)
        return send(
            FAC.at[RING * g + q, 9:11], FRY.at[g, y], fss.at[2, g, k, 0], frs.at[2, g, y, 0], dev(z, x, q, c)
        )

    def f_y_in(g, k):
        p = far(y, k)
        return send(
            FAC.at[RING * g + p, 9:11], FRY.at[g, p], fss.at[2, g, k, 0], frs.at[2, g, p, 0], dev(z, x, p, c)
        )

    def f_c(g, j):
        return send(
            FAC.at[RING * g + 2 * j + 1 - c, 8], FRC.at[g, j, c],
            fss.at[3, g, j, 0], frs.at[3, g, j, 0], dev(z, x, y, 1 - c),
        )

    def f_c_in(g, j):
        return send(
            FAC.at[RING * g + 2 * j + 1 - c, 8], FRC.at[g, j, 1 - c],
            fss.at[3, g, j, 0], frs.at[3, g, j, 0], dev(z, x, y, 1 - c),
        )

    def local(i):
        cols = pl.ds(pl.multiple_of(i * WL, WL), WL)
        for k in range(4):
            span = 2**k
            places = []
            for n in range(BLOCKS // 2):
                la = n // span * (2 * span) + n % span
                places.append((la, la + span))
            results = []
            for la, lb in places:
                results.append(
                    pair(
                        (FAC[la, k, 0], FAC[la, k, 1]), (FAC[lb, k, 0], FAC[lb, k, 1]),
                        H[la, :, cols], H[lb, :, cols],
                    )
                )
            for (la, lb), (oa, ob) in zip(places, results):
                H[la, :, cols] = oa
                H[lb, :, cols] = ob

    load_fz(0, 1).wait()
    scale(0, RING, (4, 5))
    pl.semaphore_wait(barrier, len(partners))
    for n in range(2):
        for k in HOPS:
            f_z(0, k, n).start()
    for k in range(4):
        load_f(k).wait()
    scale(0, BLOCKS, (0, 1, 2, 3))
    load_x(0).wait()
    local(0)

    def place(u):
        g, cc = lax.div(u, chunks), lax.rem(u, chunks)
        return g, pl.ds(pl.multiple_of(cc * W, W), W), lax.rem(u, DEPTH)

    def z_out(u, k):
        g, cols, d = place(u)
        q = far(z, k)
        return send(
            H.at[RING * g + q, :, cols], RZ.at[u, z], sh.at[d, k], rz.at[u, z], dev(q, x, y, c)
        )

    def z_out_in(u, k):
        p = far(z, k)
        return send(SZ.at[0, p], RZ.at[u, p], sh.at[0, k], rz.at[u, p], dev(p, x, y, c))

    def z_back(u, k):
        d = lax.rem(u, DEPTH)
        p = far(z, k)
        return send(SZ.at[d, p], HZ.at[u, z], sz.at[d, k], rh.at[u, z], dev(p, x, y, c))

    def z_back_in(u, k):
        p = far(z, k)
        return send(SZ.at[0, p], HZ.at[u, p], sz.at[0, k], rh.at[u, p], dev(p, x, y, c))

    def x_out(u, k):
        d = lax.rem(u, DEPTH)
        q = far(x, k)
        return send(HZ.at[u, q], RX.at[u, x], shx.at[d, k], rx.at[u, x], dev(z, q, y, c))

    def x_out_in(u, k):
        p = far(x, k)
        return send(SX.at[0, p], RX.at[u, p], shx.at[0, k], rx.at[u, p], dev(z, p, y, c))

    cx = lax.rem(x, 2)
    cy = lax.rem(y, 2)

    def x_back(u, k):
        d = lax.rem(u, DEPTH)
        p = far(x, k)
        return send(
            SX.at[d, p], RC.at[u, lax.div(x, 2), c], sx.at[d, k], rc.at[u, lax.div(x, 2), c],
            dev(z, p, y, cx),
        )

    def x_back_in(u, j, e):
        return send(
            SX.at[0, 0], RC.at[u, j, e], sx.at[0, 0], rc.at[u, j, e], dev(z, c + 2 * j, y, e)
        )

    def y_out(u, j, e):
        d = lax.rem(u, DEPTH)
        to = c if e == 0 else 1 - c
        return send(
            SC.at[d, j, to], RY.at[u, y], sc.at[d, j, e], ry.at[u, y], dev(z, x, c + 2 * j, to)
        )

    def y_out_in(u, k):
        p = far(y, k)
        return send(SY.at[0, p], RY.at[u, p], sc.at[0, 0, 0], ry.at[u, p], dev(z, x, p, cy))

    def y_back(u, k):
        g, cols, d = place(u)
        p = far(y, k)
        return send(
            SY.at[d, p], out.at[RING * g + y, :, cols], sy.at[d, k], ro.at[u, y], dev(z, x, p, c)
        )

    def y_back_in(u, k):
        g, cols, d = place(u)
        p = far(y, k)
        return send(
            SY.at[0, p], out.at[RING * g + p, :, cols], sy.at[0, k], ro.at[u, p], dev(z, x, p, c)
        )

    def keep(u):
        g, cols, d = place(u)
        return pltpu.make_async_copy(SY.at[d, y], out.at[RING * g + y, :, cols], os.at[d])

    def reuse(u, waits):
        @pl.when(u >= DEPTH)
        def _():
            waits(u)

    def sent(copy):
        return lambda u: [copy(u, k).wait_send() for k in HOPS]

    def x_back_sent(u):
        for k in HOPS:
            x_back(u, k).wait_send()

        @pl.when(cx != c)
        def _():
            x_back(u, 0).wait_send()

    def y_out_sent(u):
        for j in range(2):
            y_out(u, j, 1).wait_send()

            @pl.when(y != c + 2 * j)
            def _():
                y_out(u, j, 0).wait_send()

    def y_back_sent(u):
        for k in HOPS:
            y_back(u, k).wait_send()
        keep(u).wait()

    def first_chunk(u, wait):
        g, cc = lax.div(u, chunks), lax.rem(u, chunks)

        @pl.when(cc == 0)
        def _():
            wait(g)

    def two_levels(F, g, R, u):
        v = [R[u, p] for p in range(RING)]
        for level, pairs in enumerate((((0, 1), (2, 3)), ((0, 2), (1, 3)))):
            for a, b in pairs:
                v[a], v[b] = pair(
                    (F[g, a, level, 0], F[g, a, level, 1]), (F[g, b, level, 0], F[g, b, level, 1]),
                    v[a], v[b],
                )
        return v

    def stage_z_out(u):
        reuse(u, sent(z_out))
        for k in HOPS:
            z_out(u, k).start()
        g, cols, d = place(u)
        RZ[u, z] = H[RING * g + z, :, cols]
        cc = lax.rem(u, chunks)
        for i, k in enumerate(HOPS):
            for n in range(2):
                @pl.when(jnp.logical_and(g < GROUPS - 1, cc == 3 * n + i + 1))
                def _(k=k, n=n):
                    f_z(g + 1, k, n).start()

            @pl.when(jnp.logical_and(jnp.logical_and(g > 0, g < GROUPS - 1), cc == 2 * i))
            def _(k=k):
                f_x(g + 1, k).start()

    def stage_z(u):
        g, cols, d = place(u)
        first_chunk(u, lambda g: [f_z_in(g, k, n).wait_recv() for k in HOPS for n in range(2)])
        reuse(u, sent(z_back))
        for k in HOPS:
            z_out_in(u, k).wait_recv()
        v = two_levels(FRZ, g, RZ, u)
        for p in range(RING):
            SZ[d, p] = v[p]
        for k in HOPS:
            z_back(u, k).start()
        HZ[u, z] = SZ[d, z]

    def stage_x_out(u):
        reuse(u, sent(x_out))
        for k in HOPS:
            z_back_in(u, k).wait_recv()
        for k in HOPS:
            x_out(u, k).start()
        RX[u, x] = HZ[u, x]

    def stage_x(u):
        g, cols, d = place(u)
        first_chunk(u, lambda g: [f_x_in(g, k).wait_recv() for k in HOPS])
        reuse(u, x_back_sent)
        for k in HOPS:
            x_out_in(u, k).wait_recv()
        v = two_levels(FRX, g, RX, u)
        for p in range(RING):
            SX[d, p] = v[p]
        for k in HOPS:
            x_back(u, k).start()

        @pl.when(cx != c)
        def _():
            x_back(u, 0).start()

        @pl.when(cx == c)
        def _():
            RC[u, lax.div(x, 2), c] = SX[d, x]

    def stage_c(u):
        g, cols, d = place(u)
        first_chunk(u, lambda g: [f_c_in(g, j).wait_recv() for j in range(2)])
        reuse(u, y_out_sent)
        for j in range(2):
            x_back_in(u, j, 1 - c).wait_recv()

            @pl.when(x != c + 2 * j)
            def _():
                x_back_in(u, j, c).wait_recv()

        for j in range(2):
            a, b = pair(
                (FRC[g, j, 0, 0], FRC[g, j, 0, 1]), (FRC[g, j, 1, 0], FRC[g, j, 1, 1]),
                RC[u, j, 0], RC[u, j, 1],
            )
            SC[d, j, 0] = a
            SC[d, j, 1] = b
        for j in range(2):
            y_out(u, j, 1).start()

            @pl.when(y != c + 2 * j)
            def _():
                y_out(u, j, 0).start()

            @pl.when(y == c + 2 * j)
            def _():
                RY[u, y] = SC[d, j, c]

    def stage_y(u):
        g, cols, d = place(u)
        first_chunk(u, lambda g: [f_y_in(g, k).wait_recv() for k in HOPS])
        reuse(u, y_back_sent)
        for k in HOPS:
            y_out_in(u, k).wait_recv()

        @pl.when(cy != c)
        def _():
            y_out_in(u, 0).wait_recv()

        v = two_levels(FRY, g, RY, u)
        for p in range(RING):
            SY[d, p] = v[p]
        for k in HOPS:
            y_back(u, k).start()
        keep(u).start()

    stages = (stage_z_out, stage_z, stage_x_out, stage_x, stage_c, stage_y)

    def own_factors(g, carry):
        FRX[g, x] = FAC[RING * g + x, 6:8]
        FRY[g, y] = FAC[RING * g + y, 9:11]
        for j in range(2):
            FRC[g, j, c] = FAC[RING * g + 2 * j + c, 8]
        return carry

    def own_z(g, carry):
        FRZ[g, z] = FAC[RING * g + z, 4:6]
        return carry

    own_z(0, 0)

    def step(t, carry):
        for n in ORDER:
            off, stage = OFF[n], stages[n]

            @pl.when(jnp.logical_and(t >= off, t < off + units))
            def _(off=off, stage=stage):
                stage(t - off)

            if stage is stage_z_out:
                @pl.when(t == 0)
                def _():
                    load_fz(1, GROUPS - 1).wait()
                    scale(RING, BLOCKS - RING, (4, 5))
                    lax.fori_loop(1, GROUPS, own_z, 0)

                @pl.when(jnp.logical_and(t < 2 * (width // WL - 1), lax.rem(t, 2) == 0))
                def _():
                    i = lax.div(t, 2) + 1
                    load_x(i).wait()
                    local(i)

                @pl.when(t == 1)
                def _():
                    for k in range(6, 11):
                        load_f(k).wait()
                    scale(0, BLOCKS, (6, 7, 8, 9, 10))
                    for g in range(GROUPS):
                        for k in HOPS if g < 2 else ():
                            f_x(g, k).start()
                        for j in range(2):
                            f_c(g, j).start()
                        for k in HOPS:
                            f_y(g, k).start()
                    lax.fori_loop(0, GROUPS, own_factors, 0)

        return carry

    lax.fori_loop(0, units + max(OFF), step, 0)

    def last(u, carry):
        for copy in (z_out, z_back, x_out):
            sent(copy)(u)
        x_back_sent(u)
        y_out_sent(u)
        y_back_sent(u)
        return carry

    lax.fori_loop(units - DEPTH, units, last, 0)

    def finish(u, carry):
        for k in HOPS:
            y_back_in(u, k).wait_recv()
        return carry

    lax.fori_loop(0, units, finish, 0)
    for g in range(GROUPS):
        for k in HOPS:
            f_x(g, k).wait_send()
            f_y(g, k).wait_send()
            for n in range(2):
                f_z(g, k, n).wait_send()
        for j in range(2):
            f_c(g, j).wait_send()


def on_device(x_blocks, factors, pattern):
    blocks, order, width = x_blocks.shape[2:]
    levels = factors.shape[3]
    units = GROUPS * (width // W)
    dma = pltpu.SemaphoreType.DMA
    bf = jnp.bfloat16
    tile = (order, W)
    square = (order, order)
    scratch = [
        pltpu.VMEM((blocks, order, width), bf),
        pltpu.VMEM((blocks, levels, 2) + square, bf),
        pltpu.VMEM((GROUPS, RING, 2, 2) + square, bf),
        pltpu.VMEM((GROUPS, RING, 2, 2) + square, bf),
        pltpu.VMEM((GROUPS, 2, 2, 2) + square, bf),
        pltpu.VMEM((GROUPS, RING, 2, 2) + square, bf),
    ]
    scratch += [pltpu.VMEM((units, RING) + tile, bf)] * 3
    scratch += [pltpu.VMEM((units, 2, 2) + tile, bf), pltpu.VMEM((units, RING) + tile, bf)]
    scratch += [pltpu.VMEM((DEPTH, RING) + tile, bf)] * 2
    scratch += [pltpu.VMEM((DEPTH, 2, 2) + tile, bf), pltpu.VMEM((DEPTH, RING) + tile, bf)]
    scratch += [
        dma((width // WL,)), dma((levels,)), dma((4, GROUPS, RING, 2)), dma((4, GROUPS, RING, 2)),
        dma((units, RING)), dma((units, RING)), dma((units, RING)), dma((units, 2, 2)),
        dma((units, RING)), dma((units, RING)),
        dma((DEPTH, RING)), dma((DEPTH, RING)), dma((DEPTH, RING)), dma((DEPTH, RING)),
        dma((DEPTH, 2, 2)), dma((DEPTH, RING)), dma((DEPTH,)),
    ]
    result = pl.pallas_call(
        kernel,
        out_shape=jax.ShapeDtypeStruct((blocks, order, width), bf),
        in_specs=[
            pl.BlockSpec(memory_space=pltpu.SMEM),
            pl.BlockSpec(memory_space=pl.ANY),
            pl.BlockSpec(memory_space=pl.ANY),
        ],
        out_specs=pl.BlockSpec(memory_space=pl.ANY),
        scratch_shapes=scratch,
        name="butterfly",
        cost_estimate=pl.CostEstimate(
            flops=blocks * levels * 4 * order * order * width,
            bytes_accessed=2 * (2 * x_blocks.size + factors.size),
            transcendentals=0,
        ),
        compiler_params=pltpu.CompilerParams(
            collective_id=0, has_side_effects=True, vmem_limit_bytes=48 * 2**20
        ),
    )(
        jnp.transpose(pattern, (0, 3, 1, 2)),
        x_blocks.reshape(blocks, order, width),
        factors.reshape(blocks, levels, 2, order, order),
    )
    return result.reshape(1, 1, blocks, order, width)


def solution(mesh):
    return jax.shard_map(
        on_device,
        mesh=mesh,
        in_specs=(
            P("row", "col", None, None, None),
            P("row", "col", None, None, None, None, None),
            P("row", "col", None, None),
        ),
        out_specs=P("row", "col", None, None, None),
        check_vma=False,
    )
```

```python
import functools

import jax
import jax.numpy as jnp
from jax import lax
from jax.experimental import pallas as pl
from jax.experimental.pallas import tpu as pltpu
from jax.sharding import PartitionSpec as P

MESH = pl.DeviceIdType.MESH
B = 128
W = 128
WL = 256
RING = 4
BLOCKS = 16
GROUPS = BLOCKS // RING
OFF = (0, 2, 4, 6, 8, 10)
ORDER = (0, 1, 2, 3, 4, 5)


def dot(lhs, rhs):
    return jnp.dot(lhs, rhs, preferred_element_type=jnp.float32).astype(jnp.bfloat16)


def pair(fa, fb, va, vb):
    lhs = jnp.concatenate(
        [jnp.concatenate([fa[0], fa[1]], axis=1), jnp.concatenate([fb[1], fb[0]], axis=1)], axis=0
    )
    res = dot(lhs, jnp.concatenate([va, vb], axis=0))
    return res[:B], res[B:]


def kernel(
    pat, x_hbm, f_hbm, out, H, FAC, FRZ, FRX, FRC, FRY,
    RZ, HZ, RX, RC, RY,
    xs, fs, frs, fss,
    rz, rh, rx, rc, ry, ro, ss, os,
):
    width = H.shape[2]
    chunks = width // W
    units = GROUPS * chunks
    row = lax.axis_index("row")
    col = lax.axis_index("col")
    y, c = lax.div(row, 2), lax.rem(row, 2)
    x, z = lax.div(col, 4), lax.rem(col, 4)

    def dev(z_, x_, y_, c_):
        return (y_ * 2 + c_, x_ * 4 + z_)

    def far(p, k):
        return lax.rem(p + k, RING)

    HOPS = (2, 1, 3)

    def send(src, dst, ssem, rsem, to):
        return pltpu.make_async_remote_copy(
            src_ref=src, dst_ref=dst, send_sem=ssem, recv_sem=rsem, device_id=to, device_id_type=MESH
        )

    def load_f(k):
        return pltpu.make_async_copy(f_hbm.at[:, k], FAC.at[:, k], fs.at[k])

    def load_fz(g, n):
        part = pl.ds(RING * g, RING * n)
        return pltpu.make_async_copy(
            f_hbm.at[part, 4:6], FAC.at[part, 4:6], fs.at[4 if g == 0 else 5]
        )

    def load_x(i):
        cols = pl.ds(i * WL, WL)
        return pltpu.make_async_copy(x_hbm.at[:, :, cols], H.at[:, :, cols], xs.at[i])

    load_fz(0, 1).start()
    load_x(0).start()
    for k in range(4):
        load_f(k).start()

    barrier = pltpu.get_barrier_semaphore()
    partners = [dev(far(z, k), x, y, c) for k in HOPS]
    partners += [dev(z, far(x, k), y, e) for k in HOPS for e in (c, 1 - c)]
    partners += [dev(z, x, far(y, k), e) for k in HOPS for e in (c, 1 - c)]
    partners += [dev(z, x, y, 1 - c)]
    for to in partners:
        pl.semaphore_signal(barrier, inc=1, device_id=to, device_id_type=MESH)

    def scale(first, count, levels):
        def body(l, carry):
            for k in levels:
                m = pat[0, k, 0, l].astype(jnp.float32)
                FAC[l, k, 1] = (FAC[l, k, 1].astype(jnp.float32) * m).astype(jnp.bfloat16)
            return carry

        lax.fori_loop(first, first + count, body, 0)

    def waits(region, sem):
        return send(region, region, sem, sem, dev(z, x, y, 1 - c))

    def f_z(g, k, n):
        q = far(z, k)
        return send(
            FAC.at[RING * g + q, 4 + n], FRZ.at[g, z, n], fss.at[0], frs.at[0, g], dev(q, x, y, c)
        )

    def f_x(g, k):
        q = far(x, k)
        return send(
            FAC.at[RING * g + q, 6:8], FRX.at[g, x], fss.at[1], frs.at[1, g], dev(z, q, y, c)
        )

    def f_y(g, k):
        q = far(y, k)
        return send(
            FAC.at[RING * g + q, 9:11], FRY.at[g, y], fss.at[2], frs.at[2, g], dev(z, x, q, c)
        )

    def f_c(g, j):
        return send(
            FAC.at[RING * g + 2 * j + 1 - c, 8], FRC.at[g, j, c], fss.at[3], frs.at[3, g],
            dev(z, x, y, 1 - c),
        )

    def local(i):
        cols = pl.ds(pl.multiple_of(i * WL, WL), WL)
        for k in range(4):
            span = 2**k
            places = []
            for n in range(BLOCKS // 2):
                la = n // span * (2 * span) + n % span
                places.append((la, la + span))
            results = []
            for la, lb in places:
                results.append(
                    pair(
                        (FAC[la, k, 0], FAC[la, k, 1]), (FAC[lb, k, 0], FAC[lb, k, 1]),
                        H[la, :, cols], H[lb, :, cols],
                    )
                )
            for (la, lb), (oa, ob) in zip(places, results):
                H[la, :, cols] = oa
                H[lb, :, cols] = ob

    load_fz(0, 1).wait()
    scale(0, RING, (4, 5))
    pl.semaphore_wait(barrier, len(partners))
    for n in range(2):
        for k in HOPS:
            f_z(0, k, n).start()
    for k in range(4):
        load_f(k).wait()
        scale(0, BLOCKS, (k,))
    load_x(0).wait()
    load_fz(1, GROUPS - 1).start()
    for i in range(1, width // WL):
        load_x(i).start()
    for k in range(6, 11):
        load_f(k).start()
    local(0)

    def place(u):
        g, cc = lax.div(u, chunks), lax.rem(u, chunks)
        return g, pl.ds(pl.multiple_of(cc * W, W), W)

    def z_out(u, k):
        g, cols = place(u)
        q = far(z, k)
        return send(H.at[RING * g + q, :, cols], RZ.at[u, z], ss.at[0], rz.at[u], dev(q, x, y, c))

    def z_back(u, k):
        p = far(z, k)
        return send(RZ.at[u, p], HZ.at[u, z], ss.at[1], rh.at[u], dev(p, x, y, c))

    def x_out(u, k):
        q = far(x, k)
        return send(HZ.at[u, q], RX.at[u, x], ss.at[2], rx.at[u], dev(z, q, y, c))

    cx = lax.rem(x, 2)
    cy = lax.rem(y, 2)

    def x_back(u, k):
        p = far(x, k)
        return send(
            RX.at[u, p], RC.at[u, lax.div(x, 2), c], ss.at[3], rc.at[u], dev(z, p, y, cx)
        )

    def y_out(u, j, to):
        return send(RC.at[u, j, to], RY.at[u, y], ss.at[4], ry.at[u], dev(z, x, c + 2 * j, to))

    def y_back(u, k):
        g, cols = place(u)
        p = far(y, k)
        return send(
            RY.at[u, p], out.at[RING * g + y, :, cols], ss.at[5], ro, dev(z, x, p, c)
        )

    def keep(u):
        g, cols = place(u)
        return pltpu.make_async_copy(RY.at[u, y], out.at[RING * g + y, :, cols], os)

    def first_chunk(u, wait):
        g, cc = lax.div(u, chunks), lax.rem(u, chunks)

        @pl.when(cc == 0)
        def _():
            wait(g)

    def two_levels(F, g, R, u):
        v = [R[u, p] for p in range(RING)]
        for level, pairs in enumerate((((0, 1), (2, 3)), ((0, 2), (1, 3)))):
            for a, b in pairs:
                v[a], v[b] = pair(
                    (F[g, a, level, 0], F[g, a, level, 1]), (F[g, b, level, 0], F[g, b, level, 1]),
                    v[a], v[b],
                )
        for p in range(RING):
            R[u, p] = v[p]

    def stage_z_out(u):
        for k in HOPS:
            z_out(u, k).start()
        g, cols = place(u)
        RZ[u, z] = H[RING * g + z, :, cols]
        cc = lax.rem(u, chunks)
        for i, k in enumerate(HOPS):
            for n in range(2):
                @pl.when(jnp.logical_and(g < GROUPS - 1, cc == 3 * n + i + 1))
                def _(k=k, n=n):
                    f_z(g + 1, k, n).start()

            @pl.when(jnp.logical_and(jnp.logical_and(g > 0, g < GROUPS - 1), cc == 2 * i))
            def _(k=k):
                f_x(g + 1, k).start()

    def stage_z(u):
        g, cols = place(u)
        first_chunk(u, lambda g: waits(FRZ.at[g, 0 : RING - 1], frs.at[0, g]).wait_recv())
        waits(RZ.at[u, 0 : RING - 1], rz.at[u]).wait_recv()
        two_levels(FRZ, g, RZ, u)
        for k in HOPS:
            z_back(u, k).start()
        HZ[u, z] = RZ[u, z]

    def stage_x_out(u):
        waits(HZ.at[u, 0 : RING - 1], rh.at[u]).wait_recv()
        for k in HOPS:
            x_out(u, k).start()
        RX[u, x] = HZ[u, x]

    def stage_x(u):
        g, cols = place(u)
        first_chunk(u, lambda g: waits(FRX.at[g, 0 : RING - 1], frs.at[1, g]).wait_recv())
        waits(RX.at[u, 0 : RING - 1], rx.at[u]).wait_recv()
        two_levels(FRX, g, RX, u)
        for k in HOPS:
            x_back(u, k).start()

        @pl.when(cx != c)
        def _():
            x_back(u, 0).start()

        @pl.when(cx == c)
        def _():
            RC[u, lax.div(x, 2), c] = RX[u, x]

    def stage_c(u):
        g, cols = place(u)
        first_chunk(u, lambda g: waits(FRC.at[g, :, 0], frs.at[3, g]).wait_recv())

        @pl.when(cx == c)
        def _():
            waits(RX.at[u, 0 : RING - 1], rc.at[u]).wait_recv()

        @pl.when(cx != c)
        def _():
            waits(RX.at[u], rc.at[u]).wait_recv()

        for j in range(2):
            a, b = pair(
                (FRC[g, j, 0, 0], FRC[g, j, 0, 1]), (FRC[g, j, 1, 0], FRC[g, j, 1, 1]),
                RC[u, j, 0], RC[u, j, 1],
            )
            RC[u, j, 0] = a
            RC[u, j, 1] = b
        for j in range(2):
            y_out(u, j, 1 - c).start()

            @pl.when(y != c + 2 * j)
            def _():
                y_out(u, j, c).start()

            @pl.when(y == c + 2 * j)
            def _():
                RY[u, y] = RC[u, j, c]

    def stage_y(u):
        g, cols = place(u)
        first_chunk(u, lambda g: waits(FRY.at[g, 0 : RING - 1], frs.at[2, g]).wait_recv())

        @pl.when(cy == c)
        def _():
            waits(RY.at[u, 0 : RING - 1], ry.at[u]).wait_recv()

        @pl.when(cy != c)
        def _():
            waits(RY.at[u], ry.at[u]).wait_recv()

        two_levels(FRY, g, RY, u)
        for k in HOPS:
            y_back(u, k).start()
        keep(u).start()

    stages = (stage_z_out, stage_z, stage_x_out, stage_x, stage_c, stage_y)

    def own_factors(g, carry):
        FRX[g, x] = FAC[RING * g + x, 6:8]
        FRY[g, y] = FAC[RING * g + y, 9:11]
        for j in range(2):
            FRC[g, j, c] = FAC[RING * g + 2 * j + c, 8]
        return carry

    def own_z(g, carry):
        FRZ[g, z] = FAC[RING * g + z, 4:6]
        return carry

    own_z(0, 0)

    def step(t, carry):
        for n in ORDER:
            off, stage = OFF[n], stages[n]

            @pl.when(jnp.logical_and(t >= off, t < off + units))
            def _(off=off, stage=stage):
                stage(t - off)

            if stage is stage_z_out:
                @pl.when(t == 0)
                def _():
                    load_fz(1, GROUPS - 1).wait()
                    scale(RING, BLOCKS - RING, (4, 5))
                    lax.fori_loop(1, GROUPS, own_z, 0)

                @pl.when(jnp.logical_and(t < 2 * (width // WL - 1), lax.rem(t, 2) == 0))
                def _():
                    i = lax.div(t, 2) + 1
                    load_x(i).wait()
                    local(i)

                @pl.when(t == 1)
                def _():
                    for k in range(6, 11):
                        load_f(k).wait()
                    scale(0, BLOCKS, (6, 7, 8, 9, 10))
                    for g in range(GROUPS):
                        for k in HOPS if g < 2 else ():
                            f_x(g, k).start()
                        for j in range(2):
                            f_c(g, j).start()
                        for k in HOPS:
                            f_y(g, k).start()
                    lax.fori_loop(0, GROUPS, own_factors, 0)

        return carry

    lax.fori_loop(0, units + max(OFF), step, 0)

    own = RING - 1
    waits(out.at[0 : own * GROUPS], ro).wait_recv()
    pltpu.make_async_copy(out.at[0:GROUPS], out.at[0:GROUPS], os).wait()
    for n, R in enumerate((RZ, RZ, RZ)):
        waits(R.at[:, 0:own], ss.at[n]).wait_send()
    waits(RY.at[:, 0:own], ss.at[5]).wait_send()

    @pl.when(cx == c)
    def _():
        waits(RX.at[:, 0:own], ss.at[3]).wait_send()

    @pl.when(cx != c)
    def _():
        waits(RX, ss.at[3]).wait_send()

    @pl.when(cy == c)
    def _():
        waits(RX.at[:, 0:own], ss.at[4]).wait_send()

    @pl.when(cy != c)
    def _():
        waits(RX, ss.at[4]).wait_send()

    for n, F in enumerate((FRZ, FRX, FRY)):
        waits(F.at[:, 0:own], fss.at[n]).wait_send()
    waits(FRC.at[:, :, 0], fss.at[3]).wait_send()


def on_device(x_blocks, factors, pattern):
    blocks, order, width = x_blocks.shape[2:]
    levels = factors.shape[3]
    units = GROUPS * (width // W)
    dma = pltpu.SemaphoreType.DMA
    bf = jnp.bfloat16
    tile = (order, W)
    square = (order, order)
    scratch = [
        pltpu.VMEM((blocks, order, width), bf),
        pltpu.VMEM((blocks, levels, 2) + square, bf),
        pltpu.VMEM((GROUPS, RING, 2, 2) + square, bf),
        pltpu.VMEM((GROUPS, RING, 2, 2) + square, bf),
        pltpu.VMEM((GROUPS, 2, 2, 2) + square, bf),
        pltpu.VMEM((GROUPS, RING, 2, 2) + square, bf),
    ]
    scratch += [pltpu.VMEM((units, RING) + tile, bf)] * 3
    scratch += [pltpu.VMEM((units, 2, 2) + tile, bf), pltpu.VMEM((units, RING) + tile, bf)]
    scratch += [
        dma((width // WL,)), dma((levels,)), dma((4, GROUPS)), dma((4,)),
        dma((units,)), dma((units,)), dma((units,)), dma((units,)), dma((units,)), dma, dma((6,)), dma,
    ]
    result = pl.pallas_call(
        kernel,
        out_shape=jax.ShapeDtypeStruct((blocks, order, width), bf),
        in_specs=[
            pl.BlockSpec(memory_space=pltpu.SMEM),
            pl.BlockSpec(memory_space=pl.ANY),
            pl.BlockSpec(memory_space=pl.ANY),
        ],
        out_specs=pl.BlockSpec(memory_space=pl.ANY),
        scratch_shapes=scratch,
        name="butterfly",
        cost_estimate=pl.CostEstimate(
            flops=blocks * levels * 4 * order * order * width,
            bytes_accessed=2 * (2 * x_blocks.size + factors.size),
            transcendentals=0,
        ),
        compiler_params=pltpu.CompilerParams(
            collective_id=0, has_side_effects=True, vmem_limit_bytes=48 * 2**20
        ),
    )(
        jnp.transpose(pattern, (0, 3, 1, 2)),
        x_blocks.reshape(blocks, order, width),
        factors.reshape(blocks, levels, 2, order, order),
    )
    return result.reshape(1, 1, blocks, order, width)


def solution(mesh):
    return jax.shard_map(
        on_device,
        mesh=mesh,
        in_specs=(
            P("row", "col", None, None, None),
            P("row", "col", None, None, None, None, None),
            P("row", "col", None, None),
        ),
        out_specs=P("row", "col", None, None, None),
        check_vma=False,
    )
```

```python
import functools

import jax
import jax.numpy as jnp
from jax import lax
from jax.experimental import pallas as pl
from jax.experimental.pallas import tpu as pltpu
from jax.sharding import PartitionSpec as P

MESH = pl.DeviceIdType.MESH
B = 128
W = 128
WL = 256
RING = 4
BLOCKS = 16
GROUPS = BLOCKS // RING
OFF = (0, 2, 4, 6, 8, 10)
ORDER = (0, 1, 2, 3, 4, 5)


def dot(lhs, rhs):
    return jnp.dot(lhs, rhs, preferred_element_type=jnp.float32).astype(jnp.bfloat16)


def pair(fa, fb, va, vb):
    lhs = jnp.concatenate(
        [jnp.concatenate([fa[0], fa[1]], axis=1), jnp.concatenate([fb[1], fb[0]], axis=1)], axis=0
    )
    res = dot(lhs, jnp.concatenate([va, vb], axis=0))
    return res[:B], res[B:]


def kernel(
    pat, x_hbm, f_hbm, out, H, FAC, FRZ, FRX, FRC, FRY,
    RZ, HZ, RX, RC, RY,
    xs, fs, frs, fss,
    rz, rh, rx, rc, ry, ro, ss, os,
):
    width = H.shape[2]
    chunks = width // W
    units = GROUPS * chunks
    row = lax.axis_index("row")
    col = lax.axis_index("col")
    y, c = lax.div(row, 2), lax.rem(row, 2)
    x, z = lax.div(col, 4), lax.rem(col, 4)

    def dev(z_, x_, y_, c_):
        return (y_ * 2 + c_, x_ * 4 + z_)

    def far(p, k):
        return lax.rem(p + k, RING)

    HOPS = (2, 1, 3)

    def send(src, dst, ssem, rsem, to):
        return pltpu.make_async_remote_copy(
            src_ref=src, dst_ref=dst, send_sem=ssem, recv_sem=rsem, device_id=to, device_id_type=MESH
        )

    def load_f(k):
        return pltpu.make_async_copy(f_hbm.at[:, k], FAC.at[:, k], fs.at[k])

    def load_fz(g, n):
        part = pl.ds(RING * g, RING * n)
        return pltpu.make_async_copy(
            f_hbm.at[part, 4:6], FAC.at[part, 4:6], fs.at[4 if g == 0 else 5]
        )

    def load_x(i):
        cols = pl.ds(i * WL, WL)
        return pltpu.make_async_copy(x_hbm.at[:, :, cols], H.at[:, :, cols], xs.at[i])

    load_fz(0, 1).start()
    load_x(0).start()
    for k in range(4):
        load_f(k).start()

    barrier = pltpu.get_barrier_semaphore()
    partners = [dev(far(z, k), x, y, c) for k in HOPS]
    partners += [dev(z, far(x, k), y, e) for k in HOPS for e in (c, 1 - c)]
    partners += [dev(z, x, far(y, k), e) for k in HOPS for e in (c, 1 - c)]
    partners += [dev(z, x, y, 1 - c)]
    for to in partners:
        pl.semaphore_signal(barrier, inc=1, device_id=to, device_id_type=MESH)

    def scale(first, count, levels):
        def body(l, carry):
            for k in levels:
                m = pat[0, k, 0, l].astype(jnp.float32)
                FAC[l, k, 1] = (FAC[l, k, 1].astype(jnp.float32) * m).astype(jnp.bfloat16)
            return carry

        lax.fori_loop(first, first + count, body, 0)

    def waits(region, sem):
        return send(region, region, sem, sem, dev(z, x, y, 1 - c))

    def f_z(g, k, n):
        q = far(z, k)
        return send(
            FAC.at[RING * g + q, 4 + n], FRZ.at[g, z, n], fss.at[0], frs.at[0, g], dev(q, x, y, c)
        )

    def f_x(g, k):
        q = far(x, k)
        return send(
            FAC.at[RING * g + q, 6:8], FRX.at[g, x], fss.at[1], frs.at[1, g], dev(z, q, y, c)
        )

    def f_y(g, k):
        q = far(y, k)
        return send(
            FAC.at[RING * g + q, 9:11], FRY.at[g, y], fss.at[2], frs.at[2, g], dev(z, x, q, c)
        )

    def f_c(g, j):
        return send(
            FAC.at[RING * g + 2 * j + 1 - c, 8], FRC.at[g, j, c], fss.at[3], frs.at[3, g],
            dev(z, x, y, 1 - c),
        )

    def local(i):
        cols = pl.ds(pl.multiple_of(i * WL, WL), WL)
        for k in range(4):
            span = 2**k
            places = []
            for n in range(BLOCKS // 2):
                la = n // span * (2 * span) + n % span
                places.append((la, la + span))
            results = []
            for la, lb in places:
                results.append(
                    pair(
                        (FAC[la, k, 0], FAC[la, k, 1]), (FAC[lb, k, 0], FAC[lb, k, 1]),
                        H[la, :, cols], H[lb, :, cols],
                    )
                )
            for (la, lb), (oa, ob) in zip(places, results):
                H[la, :, cols] = oa
                H[lb, :, cols] = ob

    load_fz(0, 1).wait()
    scale(0, RING, (4, 5))
    pl.semaphore_wait(barrier, len(partners))
    for n in range(2):
        for k in HOPS:
            f_z(0, k, n).start()
    for k in range(4):
        load_f(k).wait()
        scale(0, BLOCKS, (k,))
    load_x(0).wait()
    load_fz(1, GROUPS - 1).start()
    for i in range(1, width // WL):
        load_x(i).start()
    for k in range(6, 11):
        load_f(k).start()
    local(0)

    def place(u):
        g, cc = lax.div(u, chunks), lax.rem(u, chunks)
        return g, pl.ds(pl.multiple_of(cc * W, W), W)

    def z_out(u, k):
        g, cols = place(u)
        q = far(z, k)
        return send(H.at[RING * g + q, :, cols], RZ.at[u, z], ss.at[0], rz.at[u], dev(q, x, y, c))

    def z_back(u, k):
        p = far(z, k)
        return send(RZ.at[u, p], HZ.at[u, z], ss.at[1], rh.at[u], dev(p, x, y, c))

    def x_out(u, k):
        q = far(x, k)
        return send(HZ.at[u, q], RX.at[u, x], ss.at[2], rx.at[u], dev(z, q, y, c))

    cx = lax.rem(x, 2)
    cy = lax.rem(y, 2)

    def x_back(u, k):
        p = far(x, k)
        return send(
            RX.at[u, p], RC.at[u, lax.div(x, 2), c], ss.at[3], rc.at[u], dev(z, p, y, cx)
        )

    def y_out(u, j, to):
        return send(RC.at[u, j, to], RY.at[u, y], ss.at[4], ry.at[u], dev(z, x, c + 2 * j, to))

    def y_back(u, k):
        g, cols = place(u)
        p = far(y, k)
        return send(
            RY.at[u, p], out.at[RING * g + y, :, cols], ss.at[5], ro, dev(z, x, p, c)
        )

    def keep(u):
        g, cols = place(u)
        return pltpu.make_async_copy(RY.at[u, y], out.at[RING * g + y, :, cols], os)

    def first_chunk(u, wait):
        g, cc = lax.div(u, chunks), lax.rem(u, chunks)

        @pl.when(cc == 0)
        def _():
            wait(g)

    def two_levels(F, g, R, u):
        v = [R[u, p] for p in range(RING)]
        for level, pairs in enumerate((((0, 1), (2, 3)), ((0, 2), (1, 3)))):
            for a, b in pairs:
                v[a], v[b] = pair(
                    (F[g, a, level, 0], F[g, a, level, 1]), (F[g, b, level, 0], F[g, b, level, 1]),
                    v[a], v[b],
                )
        for p in range(RING):
            R[u, p] = v[p]

    def stage_z_out(u):
        for k in HOPS:
            z_out(u, k).start()
        g, cols = place(u)
        RZ[u, z] = H[RING * g + z, :, cols]
        cc = lax.rem(u, chunks)
        for i, k in enumerate(HOPS):
            for n in range(2):
                @pl.when(jnp.logical_and(g < GROUPS - 1, cc == 3 * n + i + 1))
                def _(k=k, n=n):
                    f_z(g + 1, k, n).start()

            @pl.when(jnp.logical_and(jnp.logical_and(g > 0, g < GROUPS - 1), cc == 2 * i))
            def _(k=k):
                f_x(g + 1, k).start()

    def stage_z(u):
        g, cols = place(u)
        first_chunk(u, lambda g: waits(FRZ.at[g, 0 : RING - 1], frs.at[0, g]).wait_recv())
        waits(RZ.at[u, 0 : RING - 1], rz.at[u]).wait_recv()
        two_levels(FRZ, g, RZ, u)
        for k in HOPS:
            z_back(u, k).start()
        HZ[u, z] = RZ[u, z]

    def stage_x_out(u):
        waits(HZ.at[u, 0 : RING - 1], rh.at[u]).wait_recv()
        for k in HOPS:
            x_out(u, k).start()
        RX[u, x] = HZ[u, x]

    def stage_x(u):
        g, cols = place(u)
        first_chunk(u, lambda g: waits(FRX.at[g, 0 : RING - 1], frs.at[1, g]).wait_recv())
        waits(RX.at[u, 0 : RING - 1], rx.at[u]).wait_recv()
        two_levels(FRX, g, RX, u)
        for k in HOPS:
            x_back(u, k).start()

        @pl.when(cx != c)
        def _():
            x_back(u, 0).start()

        @pl.when(cx == c)
        def _():
            RC[u, lax.div(x, 2), c] = RX[u, x]

    def stage_c(u):
        g, cols = place(u)
        first_chunk(u, lambda g: waits(FRC.at[g, :, 0], frs.at[3, g]).wait_recv())

        @pl.when(cx == c)
        def _():
            waits(RX.at[u, 0 : RING - 1], rc.at[u]).wait_recv()

        @pl.when(cx != c)
        def _():
            waits(RX.at[u], rc.at[u]).wait_recv()

        for j in range(2):
            a, b = pair(
                (FRC[g, j, 0, 0], FRC[g, j, 0, 1]), (FRC[g, j, 1, 0], FRC[g, j, 1, 1]),
                RC[u, j, 0], RC[u, j, 1],
            )
            RC[u, j, 0] = a
            RC[u, j, 1] = b
        for j in range(2):
            y_out(u, j, 1 - c).start()

            @pl.when(y != c + 2 * j)
            def _():
                y_out(u, j, c).start()

            @pl.when(y == c + 2 * j)
            def _():
                RY[u, y] = RC[u, j, c]

    def stage_y(u):
        g, cols = place(u)
        first_chunk(u, lambda g: waits(FRY.at[g, 0 : RING - 1], frs.at[2, g]).wait_recv())

        @pl.when(cy == c)
        def _():
            waits(RY.at[u, 0 : RING - 1], ry.at[u]).wait_recv()

        @pl.when(cy != c)
        def _():
            waits(RY.at[u], ry.at[u]).wait_recv()

        two_levels(FRY, g, RY, u)
        for k in HOPS:
            y_back(u, k).start()
        keep(u).start()

    stages = (stage_z_out, stage_z, stage_x_out, stage_x, stage_c, stage_y)

    def own_factors(g, carry):
        FRX[g, x] = FAC[RING * g + x, 6:8]
        FRY[g, y] = FAC[RING * g + y, 9:11]
        for j in range(2):
            FRC[g, j, c] = FAC[RING * g + 2 * j + c, 8]
        return carry

    def own_z(g, carry):
        FRZ[g, z] = FAC[RING * g + z, 4:6]
        return carry

    own_z(0, 0)

    def step(t, carry):
        for n in ORDER:
            off, stage = OFF[n], stages[n]

            @pl.when(jnp.logical_and(t >= off, t < off + units))
            def _(off=off, stage=stage):
                stage(t - off)

            if stage is stage_z_out:
                @pl.when(t == 0)
                def _():
                    load_fz(1, GROUPS - 1).wait()
                    scale(RING, BLOCKS - RING, (4, 5))
                    lax.fori_loop(1, GROUPS, own_z, 0)

                @pl.when(jnp.logical_and(t < 2 * (width // WL - 1), lax.rem(t, 2) == 1))
                def _():
                    i = lax.div(t, 2) + 1
                    load_x(i).wait()
                    local(i)

            if stage is stage_z:
                @pl.when(t == 2)
                def _():
                    for k in (6, 7):
                        load_f(k).wait()
                    scale(0, BLOCKS, (6, 7))
                    for g in range(2):
                        for k in HOPS:
                            f_x(g, k).start()

                @pl.when(t == 3)
                def _():
                    for k in (8, 9, 10):
                        load_f(k).wait()
                    scale(0, BLOCKS, (8, 9, 10))
                    for g in range(GROUPS):
                        for j in range(2):
                            f_c(g, j).start()
                        for k in HOPS:
                            f_y(g, k).start()
                    lax.fori_loop(0, GROUPS, own_factors, 0)

        return carry

    lax.fori_loop(0, units + max(OFF), step, 0)

    own = RING - 1
    waits(out.at[0 : own * GROUPS], ro).wait_recv()
    pltpu.make_async_copy(out.at[0:GROUPS], out.at[0:GROUPS], os).wait()
    for n, R in enumerate((RZ, RZ, RZ)):
        waits(R.at[:, 0:own], ss.at[n]).wait_send()
    waits(RY.at[:, 0:own], ss.at[5]).wait_send()

    @pl.when(cx == c)
    def _():
        waits(RX.at[:, 0:own], ss.at[3]).wait_send()

    @pl.when(cx != c)
    def _():
        waits(RX, ss.at[3]).wait_send()

    @pl.when(cy == c)
    def _():
        waits(RX.at[:, 0:own], ss.at[4]).wait_send()

    @pl.when(cy != c)
    def _():
        waits(RX, ss.at[4]).wait_send()

    for n, F in enumerate((FRZ, FRX, FRY)):
        waits(F.at[:, 0:own], fss.at[n]).wait_send()
    waits(FRC.at[:, :, 0], fss.at[3]).wait_send()


def on_device(x_blocks, factors, pattern):
    blocks, order, width = x_blocks.shape[2:]
    levels = factors.shape[3]
    units = GROUPS * (width // W)
    dma = pltpu.SemaphoreType.DMA
    bf = jnp.bfloat16
    tile = (order, W)
    square = (order, order)
    scratch = [
        pltpu.VMEM((blocks, order, width), bf),
        pltpu.VMEM((blocks, levels, 2) + square, bf),
        pltpu.VMEM((GROUPS, RING, 2, 2) + square, bf),
        pltpu.VMEM((GROUPS, RING, 2, 2) + square, bf),
        pltpu.VMEM((GROUPS, 2, 2, 2) + square, bf),
        pltpu.VMEM((GROUPS, RING, 2, 2) + square, bf),
    ]
    scratch += [pltpu.VMEM((units, RING) + tile, bf)] * 3
    scratch += [pltpu.VMEM((units, 2, 2) + tile, bf), pltpu.VMEM((units, RING) + tile, bf)]
    scratch += [
        dma((width // WL,)), dma((levels,)), dma((4, GROUPS)), dma((4,)),
        dma((units,)), dma((units,)), dma((units,)), dma((units,)), dma((units,)), dma, dma((6,)), dma,
    ]
    result = pl.pallas_call(
        kernel,
        out_shape=jax.ShapeDtypeStruct((blocks, order, width), bf),
        in_specs=[
            pl.BlockSpec(memory_space=pltpu.SMEM),
            pl.BlockSpec(memory_space=pl.ANY),
            pl.BlockSpec(memory_space=pl.ANY),
        ],
        out_specs=pl.BlockSpec(memory_space=pl.ANY),
        scratch_shapes=scratch,
        name="butterfly",
        cost_estimate=pl.CostEstimate(
            flops=blocks * levels * 4 * order * order * width,
            bytes_accessed=2 * (2 * x_blocks.size + factors.size),
            transcendentals=0,
        ),
        compiler_params=pltpu.CompilerParams(
            collective_id=0, has_side_effects=True, vmem_limit_bytes=48 * 2**20
        ),
    )(
        jnp.transpose(pattern, (0, 3, 1, 2)),
        x_blocks.reshape(blocks, order, width),
        factors.reshape(blocks, levels, 2, order, order),
    )
    return result.reshape(1, 1, blocks, order, width)


def solution(mesh):
    return jax.shard_map(
        on_device,
        mesh=mesh,
        in_specs=(
            P("row", "col", None, None, None),
            P("row", "col", None, None, None, None, None),
            P("row", "col", None, None),
        ),
        out_specs=P("row", "col", None, None, None),
        check_vma=False,
    )
```

```python
import functools

import jax
import jax.numpy as jnp
from jax import lax
from jax.experimental import pallas as pl
from jax.experimental.pallas import tpu as pltpu
from jax.sharding import PartitionSpec as P

MESH = pl.DeviceIdType.MESH
B = 128
W = 128
WL = 256
RING = 4
BLOCKS = 16
GROUPS = BLOCKS // RING
OFF = (0, 2, 4, 6, 8, 10)
ORDER = (0, 1, 2, 3, 4, 5)


def dot(lhs, rhs):
    return jnp.dot(lhs, rhs, preferred_element_type=jnp.float32).astype(jnp.bfloat16)


def pair(fa, fb, va, vb):
    lhs = jnp.concatenate(
        [jnp.concatenate([fa[0], fa[1]], axis=1), jnp.concatenate([fb[1], fb[0]], axis=1)], axis=0
    )
    res = dot(lhs, jnp.concatenate([va, vb], axis=0))
    return res[:B], res[B:]


def kernel(
    pat, x_hbm, f_hbm, out, H, FAC, FRZ, FRX, FRC, FRY,
    RZ, HZ, RX, RC, RY,
    xs, fs, frs, fss,
    rz, rh, rx, rc, ry, ro, ss, os,
):
    width = H.shape[2]
    chunks = width // W
    units = GROUPS * chunks
    row = lax.axis_index("row")
    col = lax.axis_index("col")
    y, c = lax.div(row, 2), lax.rem(row, 2)
    x, z = lax.div(col, 4), lax.rem(col, 4)

    def dev(z_, x_, y_, c_):
        return (y_ * 2 + c_, x_ * 4 + z_)

    def far(p, k):
        return lax.rem(p + k, RING)

    HOPS = (2, 1, 3)

    def send(src, dst, ssem, rsem, to):
        return pltpu.make_async_remote_copy(
            src_ref=src, dst_ref=dst, send_sem=ssem, recv_sem=rsem, device_id=to, device_id_type=MESH
        )

    def load_f(k):
        return pltpu.make_async_copy(f_hbm.at[:, k], FAC.at[:, k], fs.at[k])

    def load_fz(g, n):
        part = pl.ds(RING * g, RING * n)
        return pltpu.make_async_copy(
            f_hbm.at[part, 4:6], FAC.at[part, 4:6], fs.at[4 if g == 0 else 5]
        )

    def load_x(i):
        cols = pl.ds(i * WL, WL)
        return pltpu.make_async_copy(x_hbm.at[:, :, cols], H.at[:, :, cols], xs.at[i])

    load_fz(0, 1).start()
    load_x(0).start()
    for k in range(4):
        load_f(k).start()

    barrier = pltpu.get_barrier_semaphore()
    partners = [dev(far(z, k), x, y, c) for k in HOPS]
    partners += [dev(z, far(x, k), y, e) for k in HOPS for e in (c, 1 - c)]
    partners += [dev(z, x, far(y, k), e) for k in HOPS for e in (c, 1 - c)]
    partners += [dev(z, x, y, 1 - c)]
    for to in partners:
        pl.semaphore_signal(barrier, inc=1, device_id=to, device_id_type=MESH)

    def scale(first, count, levels):
        def body(l, carry):
            for k in levels:
                m = pat[0, k, 0, l].astype(jnp.float32)
                FAC[l, k, 1] = (FAC[l, k, 1].astype(jnp.float32) * m).astype(jnp.bfloat16)
            return carry

        lax.fori_loop(first, first + count, body, 0)

    def waits(region, sem):
        return send(region, region, sem, sem, dev(z, x, y, 1 - c))

    def f_z(g, k, n):
        q = far(z, k)
        return send(
            FAC.at[RING * g + q, 4 + n], FRZ.at[g, z, n], fss.at[0], frs.at[0, g], dev(q, x, y, c)
        )

    def f_x(g, k, n):
        q = far(x, k)
        return send(
            FAC.at[RING * g + q, 6 + n], FRX.at[g, x, n], fss.at[1], frs.at[1, g], dev(z, q, y, c)
        )

    def f_y(g, k):
        q = far(y, k)
        return send(
            FAC.at[RING * g + q, 9:11], FRY.at[g, y], fss.at[2], frs.at[2, g], dev(z, x, q, c)
        )

    def f_c(g, j):
        return send(
            FAC.at[RING * g + 2 * j + 1 - c, 8], FRC.at[g, j, c], fss.at[3], frs.at[3, g],
            dev(z, x, y, 1 - c),
        )

    def local(i):
        cols = pl.ds(pl.multiple_of(i * WL, WL), WL)
        for k in range(4):
            span = 2**k
            places = []
            for n in range(BLOCKS // 2):
                la = n // span * (2 * span) + n % span
                places.append((la, la + span))
            results = []
            for la, lb in places:
                results.append(
                    pair(
                        (FAC[la, k, 0], FAC[la, k, 1]), (FAC[lb, k, 0], FAC[lb, k, 1]),
                        H[la, :, cols], H[lb, :, cols],
                    )
                )
            for (la, lb), (oa, ob) in zip(places, results):
                H[la, :, cols] = oa
                H[lb, :, cols] = ob

    load_fz(0, 1).wait()
    scale(0, RING, (4, 5))
    pl.semaphore_wait(barrier, len(partners))
    for n in range(2):
        for k in HOPS:
            f_z(0, k, n).start()
    for k in range(4):
        load_f(k).wait()
        scale(0, BLOCKS, (k,))
    load_x(0).wait()
    load_fz(1, GROUPS - 1).start()
    for i in range(1, width // WL):
        load_x(i).start()
    for k in range(6, 11):
        load_f(k).start()
    local(0)

    def place(u):
        g, cc = lax.div(u, chunks), lax.rem(u, chunks)
        return g, pl.ds(pl.multiple_of(cc * W, W), W)

    def z_out(u, k):
        g, cols = place(u)
        q = far(z, k)
        return send(H.at[RING * g + q, :, cols], RZ.at[u, z], ss.at[0], rz.at[u], dev(q, x, y, c))

    def z_back(u, k):
        p = far(z, k)
        return send(RZ.at[u, p], HZ.at[u, z], ss.at[1], rh.at[u], dev(p, x, y, c))

    def x_out(u, k):
        q = far(x, k)
        return send(HZ.at[u, q], RX.at[u, x], ss.at[2], rx.at[u], dev(z, q, y, c))

    cx = lax.rem(x, 2)
    cy = lax.rem(y, 2)

    def x_back(u, k):
        p = far(x, k)
        return send(
            RX.at[u, p], RC.at[u, lax.div(x, 2), c], ss.at[3], rc.at[u], dev(z, p, y, cx)
        )

    def y_out(u, j, to):
        return send(RC.at[u, j, to], RY.at[u, y], ss.at[4], ry.at[u], dev(z, x, c + 2 * j, to))

    def y_back(u, k):
        g, cols = place(u)
        p = far(y, k)
        return send(
            RY.at[u, p], out.at[RING * g + y, :, cols], ss.at[5], ro, dev(z, x, p, c)
        )

    def keep(u):
        g, cols = place(u)
        return pltpu.make_async_copy(RY.at[u, y], out.at[RING * g + y, :, cols], os)

    def first_chunk(u, wait):
        g, cc = lax.div(u, chunks), lax.rem(u, chunks)

        @pl.when(cc == 0)
        def _():
            wait(g)

    def two_levels(F, g, R, u):
        v = [R[u, p] for p in range(RING)]
        for level, pairs in enumerate((((0, 1), (2, 3)), ((0, 2), (1, 3)))):
            for a, b in pairs:
                v[a], v[b] = pair(
                    (F[g, a, level, 0], F[g, a, level, 1]), (F[g, b, level, 0], F[g, b, level, 1]),
                    v[a], v[b],
                )
        for p in range(RING):
            R[u, p] = v[p]

    def stage_z_out(u):
        for k in HOPS:
            z_out(u, k).start()
        g, cols = place(u)
        RZ[u, z] = H[RING * g + z, :, cols]
        cc = lax.rem(u, chunks)
        for i, k in enumerate(HOPS):
            for n in range(2):
                @pl.when(jnp.logical_and(g < GROUPS - 1, cc == 3 * n + i + 1))
                def _(k=k, n=n):
                    f_z(g + 1, k, n).start()

                    @pl.when(g > 0)
                    def _():
                        f_x(g + 1, k, n).start()


    def stage_z(u):
        g, cols = place(u)
        first_chunk(u, lambda g: waits(FRZ.at[g, 0 : RING - 1], frs.at[0, g]).wait_recv())
        waits(RZ.at[u, 0 : RING - 1], rz.at[u]).wait_recv()
        two_levels(FRZ, g, RZ, u)
        for k in HOPS:
            z_back(u, k).start()
        HZ[u, z] = RZ[u, z]

    def stage_x_out(u):
        waits(HZ.at[u, 0 : RING - 1], rh.at[u]).wait_recv()
        for k in HOPS:
            x_out(u, k).start()
        RX[u, x] = HZ[u, x]

    def stage_x(u):
        g, cols = place(u)
        first_chunk(u, lambda g: waits(FRX.at[g, 0 : RING - 1], frs.at[1, g]).wait_recv())
        waits(RX.at[u, 0 : RING - 1], rx.at[u]).wait_recv()
        two_levels(FRX, g, RX, u)
        for k in HOPS:
            x_back(u, k).start()

        @pl.when(cx != c)
        def _():
            x_back(u, 0).start()

        @pl.when(cx == c)
        def _():
            RC[u, lax.div(x, 2), c] = RX[u, x]

    def stage_c(u):
        g, cols = place(u)
        first_chunk(u, lambda g: waits(FRC.at[g, :, 0], frs.at[3, g]).wait_recv())

        @pl.when(cx == c)
        def _():
            waits(RX.at[u, 0 : RING - 1], rc.at[u]).wait_recv()

        @pl.when(cx != c)
        def _():
            waits(RX.at[u], rc.at[u]).wait_recv()

        for j in range(2):
            a, b = pair(
                (FRC[g, j, 0, 0], FRC[g, j, 0, 1]), (FRC[g, j, 1, 0], FRC[g, j, 1, 1]),
                RC[u, j, 0], RC[u, j, 1],
            )
            RC[u, j, 0] = a
            RC[u, j, 1] = b
        for j in range(2):
            y_out(u, j, 1 - c).start()

            @pl.when(y != c + 2 * j)
            def _():
                y_out(u, j, c).start()

            @pl.when(y == c + 2 * j)
            def _():
                RY[u, y] = RC[u, j, c]

    def stage_y(u):
        g, cols = place(u)
        first_chunk(u, lambda g: waits(FRY.at[g, 0 : RING - 1], frs.at[2, g]).wait_recv())

        @pl.when(cy == c)
        def _():
            waits(RY.at[u, 0 : RING - 1], ry.at[u]).wait_recv()

        @pl.when(cy != c)
        def _():
            waits(RY.at[u], ry.at[u]).wait_recv()

        two_levels(FRY, g, RY, u)
        for k in HOPS:
            y_back(u, k).start()
        keep(u).start()

    stages = (stage_z_out, stage_z, stage_x_out, stage_x, stage_c, stage_y)

    def own_factors(g, carry):
        FRX[g, x] = FAC[RING * g + x, 6:8]
        FRY[g, y] = FAC[RING * g + y, 9:11]
        for j in range(2):
            FRC[g, j, c] = FAC[RING * g + 2 * j + c, 8]
        return carry

    def own_z(g, carry):
        FRZ[g, z] = FAC[RING * g + z, 4:6]
        return carry

    own_z(0, 0)

    def step(t, carry):
        for n in ORDER:
            off, stage = OFF[n], stages[n]

            @pl.when(jnp.logical_and(t >= off, t < off + units))
            def _(off=off, stage=stage):
                stage(t - off)

            if stage is stage_z_out:
                @pl.when(t == 0)
                def _():
                    load_fz(1, GROUPS - 1).wait()
                    scale(RING, BLOCKS - RING, (4, 5))
                    lax.fori_loop(1, GROUPS, own_z, 0)

                @pl.when(jnp.logical_and(t < 2 * (width // WL - 1), lax.rem(t, 2) == 1))
                def _():
                    i = lax.div(t, 2) + 1
                    load_x(i).wait()
                    local(i)

            if stage is stage_z:
                @pl.when(t == 2)
                def _():
                    for k in (6, 7):
                        load_f(k).wait()
                    scale(0, BLOCKS, (6, 7))
                    for g in range(2):
                        for k in HOPS:
                            for n in range(2):
                                f_x(g, k, n).start()

                @pl.when(t == 3)
                def _():
                    for k in (8, 9, 10):
                        load_f(k).wait()
                    scale(0, BLOCKS, (8, 9, 10))
                    for g in range(GROUPS):
                        for j in range(2):
                            f_c(g, j).start()
                        for k in HOPS:
                            f_y(g, k).start()
                    lax.fori_loop(0, GROUPS, own_factors, 0)

        return carry

    lax.fori_loop(0, units + max(OFF), step, 0)

    own = RING - 1
    waits(out.at[0 : own * GROUPS], ro).wait_recv()
    pltpu.make_async_copy(out.at[0:GROUPS], out.at[0:GROUPS], os).wait()
    for n, R in enumerate((RZ, RZ, RZ)):
        waits(R.at[:, 0:own], ss.at[n]).wait_send()
    waits(RY.at[:, 0:own], ss.at[5]).wait_send()

    @pl.when(cx == c)
    def _():
        waits(RX.at[:, 0:own], ss.at[3]).wait_send()

    @pl.when(cx != c)
    def _():
        waits(RX, ss.at[3]).wait_send()

    @pl.when(cy == c)
    def _():
        waits(RX.at[:, 0:own], ss.at[4]).wait_send()

    @pl.when(cy != c)
    def _():
        waits(RX, ss.at[4]).wait_send()

    for n, F in enumerate((FRZ, FRX, FRY)):
        waits(F.at[:, 0:own], fss.at[n]).wait_send()
    waits(FRC.at[:, :, 0], fss.at[3]).wait_send()


def on_device(x_blocks, factors, pattern):
    blocks, order, width = x_blocks.shape[2:]
    levels = factors.shape[3]
    units = GROUPS * (width // W)
    dma = pltpu.SemaphoreType.DMA
    bf = jnp.bfloat16
    tile = (order, W)
    square = (order, order)
    scratch = [
        pltpu.VMEM((blocks, order, width), bf),
        pltpu.VMEM((blocks, levels, 2) + square, bf),
        pltpu.VMEM((GROUPS, RING, 2, 2) + square, bf),
        pltpu.VMEM((GROUPS, RING, 2, 2) + square, bf),
        pltpu.VMEM((GROUPS, 2, 2, 2) + square, bf),
        pltpu.VMEM((GROUPS, RING, 2, 2) + square, bf),
    ]
    scratch += [pltpu.VMEM((units, RING) + tile, bf)] * 3
    scratch += [pltpu.VMEM((units, 2, 2) + tile, bf), pltpu.VMEM((units, RING) + tile, bf)]
    scratch += [
        dma((width // WL,)), dma((levels,)), dma((4, GROUPS)), dma((4,)),
        dma((units,)), dma((units,)), dma((units,)), dma((units,)), dma((units,)), dma, dma((6,)), dma,
    ]
    result = pl.pallas_call(
        kernel,
        out_shape=jax.ShapeDtypeStruct((blocks, order, width), bf),
        in_specs=[
            pl.BlockSpec(memory_space=pltpu.SMEM),
            pl.BlockSpec(memory_space=pl.ANY),
            pl.BlockSpec(memory_space=pl.ANY),
        ],
        out_specs=pl.BlockSpec(memory_space=pl.ANY),
        scratch_shapes=scratch,
        name="butterfly",
        cost_estimate=pl.CostEstimate(
            flops=blocks * levels * 4 * order * order * width,
            bytes_accessed=2 * (2 * x_blocks.size + factors.size),
            transcendentals=0,
        ),
        compiler_params=pltpu.CompilerParams(
            collective_id=0, has_side_effects=True, vmem_limit_bytes=48 * 2**20
        ),
    )(
        jnp.transpose(pattern, (0, 3, 1, 2)),
        x_blocks.reshape(blocks, order, width),
        factors.reshape(blocks, levels, 2, order, order),
    )
    return result.reshape(1, 1, blocks, order, width)


def solution(mesh):
    return jax.shard_map(
        on_device,
        mesh=mesh,
        in_specs=(
            P("row", "col", None, None, None),
            P("row", "col", None, None, None, None, None),
            P("row", "col", None, None),
        ),
        out_specs=P("row", "col", None, None, None),
        check_vma=False,
    )
```
